256 devices in a mesh: heads: 8 (over z), seq: 32 (over x, y, core).
Axes of the slice: x: 4, y: 4, z: 8, core: 2. Of those that a mesh axis runs over, the one named last changes fastest.
Arguments:
- request_embeddings: bfloat16 [65536, 4096], P('seq', 'heads'), may hold values from -72 to 72
- attended_content_pile: bfloat16 [2, 65536, 4096], P(None, 'seq', 'heads'), may hold values from -4 to 4
- softness_progression: float32 [8], replicated, may hold values from 0.5 to 2
- segment_partner_chart: int32 [8, 512], P('heads'), may hold values from 0 to 511, as said below
Outputs:
- attended: bfloat16 [65536, 4096], P('seq', 'heads')
- entropy: float32 [32, 512], P('heads', 'seq')
The draws below stay inside these ranges and needn't reach their ends.
Inputs may be any that keep to these rules, and one draw needn't show every extreme that they name: Each row of segment_partner_chart is a permutation of the 512 blocks; block j is held by index j // 16 of seq. In each row, of the 16 query blocks of one index of seq, at most 1 are matched to blocks held by any one index of seq, and this count is reached.
All inputs are finite; a program needn't handle non-finite values.
Results may differ from the reference program's by a relative error of at most 0.0043.
Values may be sent and summed in bfloat16 or wider, within the bound.
A program may use at most 128 MiB of HBM per device.

```python
import math
import jax
import jax.numpy as jnp
from jax import lax

HEADS = 32
HEAD_DIM = 128
BLOCK = 128
GROUP_HEADS = 4
REFIT_REPEATS = 8
WIDTH = 4096
GROUPS = 8
TOKENS = 65536
BLOCKS_DEV = 16
REACH_SEGMENTS = 512
N_SEQ = 32


def joint_fields(key):
    request_embeddings = jnp.clip(jax.random.normal(jax.random.fold_in(key, 11), (TOKENS, WIDTH), jnp.float32), -4.0, 4.0)
    keys_field = jnp.clip(jax.random.normal(jax.random.fold_in(key, 12), (TOKENS, WIDTH), jnp.float32), -4.0, 4.0)
    values_field = jnp.clip(jax.random.normal(jax.random.fold_in(key, 13), (TOKENS, WIDTH), jnp.float32), -4.0, 4.0)
    trend = 2.0 * jnp.arange(REACH_SEGMENTS, dtype=jnp.float32) / max(REACH_SEGMENTS - 1, 1) - 1.0
    rough = jax.random.uniform(jax.random.fold_in(key, 14), (REACH_SEGMENTS,), jnp.float32, -1.0, 1.0)
    level = jnp.repeat(0.7 * trend + 0.3 * rough, BLOCK)
    direction = jnp.where(jax.random.bernoulli(jax.random.fold_in(key, 15), 0.5, (WIDTH,)), 1.0, -1.0).astype(jnp.float32)
    request_embeddings = request_embeddings + 2.0 / math.sqrt(BLOCK) * level[:, None] * direction[None, :]
    return (request_embeddings, keys_field, values_field)


def draw_request_embeddings(key, part):
    return joint_fields(key)[0].astype(jnp.bfloat16)


def draw_attended_content_pile(key, part):
    fields = joint_fields(key)
    return jnp.stack([fields[1], fields[2]], axis=0).astype(jnp.bfloat16)


def draw_softness_progression(key, part):
    key = jax.random.fold_in(key, 21)
    logs = jax.random.uniform(jax.random.fold_in(key, 1), (REFIT_REPEATS,), jnp.float32, math.log(0.5), math.log(2.0))
    first = jax.random.uniform(jax.random.fold_in(key, 2), (), jnp.float32, math.log(0.5), math.log(0.6))
    logs = logs.at[0].set(first)
    return jnp.exp(logs).astype(jnp.float32)


def draw_segment_partner_chart(key, part):
    rows_out = []
    block_index = jnp.arange(BLOCKS_DEV, dtype=jnp.int32)
    for group in range(GROUPS):
        group_key = jax.random.fold_in(key, 100 + group)
        order = jax.random.permutation(jax.random.fold_in(group_key, 1), N_SEQ).astype(jnp.int32)
        offsets_all = jax.random.permutation(jax.random.fold_in(group_key, 2), N_SEQ).astype(jnp.int32)
        offsets = offsets_all[block_index % N_SEQ]
        places = jnp.zeros((N_SEQ,), jnp.int32).at[order].set(jnp.arange(N_SEQ, dtype=jnp.int32))
        target = order[(places[:, None] + offsets[None, :]) % N_SEQ]
        slot_keys = jax.random.split(jax.random.fold_in(group_key, 3), N_SEQ)
        slot_table = jax.vmap(lambda single_key: jax.random.permutation(single_key, BLOCKS_DEV).astype(jnp.int32))(slot_keys)
        key_slot = slot_table[target, block_index[None, :]]
        matched = target * BLOCKS_DEV + key_slot
        shuffle_keys = jax.random.split(jax.random.fold_in(group_key, 4), N_SEQ)
        shuffle = jax.vmap(lambda single_key: jax.random.permutation(single_key, BLOCKS_DEV).astype(jnp.int32))(shuffle_keys)
        matched = jnp.take_along_axis(matched, shuffle, axis=1)
        rows_out.append(matched.reshape(REACH_SEGMENTS))
    return jnp.stack(rows_out, axis=0).astype(jnp.int32)


def setup_inputs(seed: int = 0) -> dict:
    arg_keys = jax.random.split(jax.random.key(seed), 5)
    return {
        "request_embeddings": draw_request_embeddings(jax.random.fold_in(arg_keys[4], 71), 0),
        "attended_content_pile": draw_attended_content_pile(jax.random.fold_in(arg_keys[4], 71), 0),
        "softness_progression": draw_softness_progression(jax.random.fold_in(arg_keys[4], 71), 0),
        "segment_partner_chart": draw_segment_partner_chart(jax.random.fold_in(arg_keys[4], 71), 0),
    }


def exponent_refit_routine(pairing_expense, softness_progression):
    column_dual_variable = jnp.zeros((pairing_expense.shape[1],), jnp.float32)
    source_dual_variable = jnp.zeros((pairing_expense.shape[0],), jnp.float32)
    chilled_charge_array = pairing_expense
    for repeat_ordinal in range(REFIT_REPEATS):
        chilled_charge_array = pairing_expense / softness_progression[repeat_ordinal]
        source_dual_variable = -jax.nn.logsumexp(chilled_charge_array + column_dual_variable[None, :], axis=1)
        column_dual_variable = -jax.nn.logsumexp(chilled_charge_array + source_dual_variable[:, None], axis=0)
    return chilled_charge_array + source_dual_variable[:, None] + column_dual_variable[None, :]

def part_stats(queries_five, keys_five, values_five):
    scores = jnp.einsum('mqgha,mkgha->mghqk', queries_five.astype(jnp.float32), keys_five.astype(jnp.float32)) * HEAD_DIM ** (-0.5)
    row_max = lax.optimization_barrier(jnp.max(scores, axis=-1))
    exponent = jnp.exp(scores - row_max[..., None])
    totals = lax.optimization_barrier(jnp.sum(exponent, axis=-1))
    moments = lax.optimization_barrier(jnp.sum(exponent * scores, axis=-1))
    weights = exponent.astype(jnp.bfloat16)
    numerator = jnp.einsum('mghqk,mkgha->mqgha', weights.astype(jnp.float32), values_five.astype(jnp.float32))
    return (numerator, row_max, totals, moments)

def combine_parts(local_part, matched_part, bias):
    numer_local, max_local, total_local, moment_local = local_part
    numer_matched, max_matched, total_matched, moment_matched = matched_part
    bias_wide = bias[:, :, None, None]
    shifted = max_matched + bias_wide
    moment_shift = moment_matched + bias_wide * total_matched
    joint = jnp.maximum(max_local, shifted)
    weight_local = jnp.exp(max_local - joint)
    weight_matched = jnp.exp(shifted - joint)
    denominator = total_local * weight_local + total_matched * weight_matched
    entropy_rows = jnp.log(denominator) + joint - (moment_local * weight_local + moment_shift * weight_matched) / denominator
    share_local = jnp.transpose(weight_local / denominator, (0, 3, 1, 2))[..., None]
    share_matched = jnp.transpose(weight_matched / denominator, (0, 3, 1, 2))[..., None]
    mixed = numer_local * share_local + numer_matched * share_matched
    return (mixed, lax.optimization_barrier(jnp.mean(entropy_rows, axis=-1)))

def reference(request_embeddings, attended_content_pile, softness_progression, segment_partner_chart):
    price_multiplier = 1.0 / (BLOCK * math.sqrt(HEAD_DIM * HEADS))
    query_sums = lax.optimization_barrier(jnp.sum(request_embeddings.reshape(REACH_SEGMENTS, BLOCK, WIDTH), axis=1, dtype=jnp.float32))
    key_sums = lax.optimization_barrier(jnp.sum(attended_content_pile[0].reshape(REACH_SEGMENTS, BLOCK, WIDTH), axis=1, dtype=jnp.float32))
    pairing_expense = jnp.dot(query_sums, key_sums.T, precision=lax.Precision.HIGHEST) * price_multiplier
    exponent_joint_density = exponent_refit_routine(pairing_expense, softness_progression) + math.log(REACH_SEGMENTS)
    query_blocks = request_embeddings.reshape(REACH_SEGMENTS, BLOCK, GROUPS, GROUP_HEADS, HEAD_DIM)
    kv_blocks = attended_content_pile.reshape(2, REACH_SEGMENTS, BLOCK, GROUPS, GROUP_HEADS, HEAD_DIM)
    outputs = []
    entropies = []
    for group in range(GROUPS):
        group_queries = query_blocks[:, :, group:group + 1]
        group_keys = kv_blocks[0, :, :, group:group + 1]
        group_values = kv_blocks[1, :, :, group:group + 1]
        order = segment_partner_chart[group].astype(jnp.int32)
        local_part = part_stats(group_queries, group_keys, group_values)
        matched_part = part_stats(group_queries, jnp.take(group_keys, order, axis=0), jnp.take(group_values, order, axis=0))
        bias = jnp.take_along_axis(exponent_joint_density, order[:, None], axis=1)
        mixed, entropy_block = combine_parts(local_part, matched_part, bias)
        outputs.append(mixed)
        entropies.append(entropy_block)
    attended = jnp.concatenate(outputs, axis=2).reshape(TOKENS, WIDTH).astype(jnp.bfloat16)
    entropy = jnp.concatenate(entropies, axis=1).reshape(REACH_SEGMENTS, HEADS).T
    return (attended, entropy)
```

```python
import math

import jax
import jax.numpy as jnp
from jax import lax
from jax.experimental import pallas as pl
from jax.experimental.pallas import tpu as pltpu
from jax.sharding import PartitionSpec as P

HEADS = 32
HEAD_DIM = 128
BLOCK = 128
GROUP_HEADS = 4
REFIT_REPEATS = 8
WIDTH = GROUP_HEADS * HEAD_DIM
BLOCKS_DEV = 16
N_SEQ = 32
N_HEADS = 8
ALL_BLOCKS = BLOCKS_DEV * N_SEQ
MESH = pl.DeviceIdType.MESH
F32 = jnp.float32
PRICE = 1.0 / (BLOCK * math.sqrt(HEAD_DIM * HEADS))
SCALE = HEAD_DIM ** (-0.5)
WANTED, QUERY, COLUMN, OWNER = range(4)


def split_slot(t):
    return t // 8, (t // 2) % 4, t % 2


def kernel(
    route, soft, q_ref, kv_ref, att_ref, ent_ref,
    pack_k, pack_v, mid_k, mid_v, fin_k, fin_v, out_slot, ent_slot,
    q_sum, k_sum, part, part_in, cost, row_pot, col_pot, mine,
    sum_send, sum_recv, red_send, red_recv, tile_send, tile_recv,
    first_k_send, first_v_send, mid_k_recv, mid_v_recv,
    second_k_send, second_v_send, fin_k_recv, fin_v_recv,
):
    seq = lax.axis_index("seq")
    z = lax.axis_index("heads")
    x, y, c = seq // 8, (seq // 2) % 4, seq % 2
    yc = seq % 8

    def place(dx, dy, dc):
        return lax.rem(x + dx, 4) * 8 + lax.rem(y + dy, 4) * 2 + lax.rem(c + dc, 2)

    def device(dx, dy, dc):
        return (z, place(dx, dy, dc))

    def floor(dz):
        return (lax.rem(z + dz, N_HEADS), seq)

    def remote(src, dst, send, recv, to):
        return pltpu.make_async_remote_copy(
            src_ref=src, dst_ref=dst, send_sem=send, recv_sem=recv, device_id=to, device_id_type=MESH
        )

    barrier = pltpu.get_barrier_semaphore()
    peers = [device(d, 0, e) for d in (1, 2, 3) for e in (0, 1)]
    peers += [device(0, d, e) for d in (1, 2, 3) for e in (0, 1)]
    peers += [device(0, 0, 1)] + [floor(d) for d in range(1, N_HEADS)]
    for peer in peers:
        pl.semaphore_signal(barrier, inc=1, device_id=peer, device_id_type=MESH)

    tokens = BLOCKS_DEV * BLOCK
    owner = lax.broadcasted_iota(jnp.int32, (BLOCKS_DEV, tokens), 1) // BLOCK
    ones = jnp.where(owner == lax.broadcasted_iota(jnp.int32, (BLOCKS_DEV, tokens), 0), 1.0, 0.0).astype(jnp.bfloat16)
    q_rows = pl.ds(pl.multiple_of(x * BLOCKS_DEV, BLOCKS_DEV), BLOCKS_DEV)
    k_rows = pl.ds(pl.multiple_of(yc * BLOCKS_DEV, BLOCKS_DEV), BLOCKS_DEV)
    q_sum[q_rows, :] = jnp.dot(ones, q_ref[...].reshape(tokens, WIDTH), preferred_element_type=F32)
    k_sum[k_rows, :] = jnp.dot(ones, kv_ref[0].reshape(tokens, WIDTH), preferred_element_type=F32)

    pl.semaphore_wait(barrier, len(peers))

    sums = []
    for d in (1, 2, 3):
        sums.append(remote(q_sum.at[q_rows], q_sum.at[q_rows], sum_send.at[d], sum_recv.at[d], device(d, 0, 0)))
    for r in range(1, 8):
        sums.append(
            remote(k_sum.at[k_rows], k_sum.at[k_rows], sum_send.at[3 + r], sum_recv.at[3 + r], device(0, r // 2, r % 2))
        )
    for copy in sums:
        copy.start()

    def first_k(t, final):
        dst, recv = (fin_k, fin_k_recv) if final else (mid_k, mid_k_recv)
        return remote(pack_k.at[t], dst.at[t], first_k_send.at[t], recv.at[t], device(t // 8, 0, 0))

    def first_v(t, final):
        dst, recv = (fin_v, fin_v_recv) if final else (mid_v, mid_v_recv)
        return remote(pack_v.at[t], dst.at[t], first_v_send.at[t], recv.at[t], device(0, (t // 2) % 4, 0))

    def second_k(t, direct):
        src = pack_k if direct else mid_k
        _, dy, dc = split_slot(t)
        return remote(src.at[t], fin_k.at[t], second_k_send.at[t], fin_k_recv.at[t], device(0, dy, dc))

    def second_v(t, direct):
        src = pack_v if direct else mid_v
        dx, _, dc = split_slot(t)
        return remote(src.at[t], fin_v.at[t], second_v_send.at[t], fin_v_recv.at[t], device(dx, 0, dc))

    def rest_k(d):
        return lambda u: d * 8 + 1 + u

    def rest_v(d):
        def slot(u):
            w = u + 1
            return (w // 2) * 8 + d * 2 + w % 2

        return slot

    def each(count, action):
        def step(u, carry):
            action(u)
            return carry

        lax.fori_loop(0, count, step, 0)

    def fill_k(t, into):
        into[t] = kv_ref[0, route[WANTED, place(*split_slot(t))]]

    def fill_v(t, into):
        into[t] = kv_ref[1, route[WANTED, place(*split_slot(t))]]

    for d in (2, 1, 3):
        def start_k(u, d=d):
            t = rest_k(d)(u)
            fill_k(t, pack_k)
            first_k(t, False).start()

        def start_v(u, d=d):
            t = rest_v(d)(u)
            fill_v(t, pack_v)
            first_v(t, False).start()

        each(7, start_k)
        each(7, start_v)
    for d in (2, 1, 3):
        fill_k(d * 8, pack_k)
        first_k(d * 8, True).start()
        fill_v(d * 2, pack_v)
        first_v(d * 2, True).start()

    fill_k(0, fin_k)
    fill_v(0, fin_v)

    def start_near_k(u):
        t = rest_k(0)(u)
        fill_k(t, pack_k)
        second_k(t, True).start()

    def start_near_v(u):
        t = rest_v(0)(u)
        fill_v(t, pack_v)
        second_v(t, True).start()

    for copy in sums:
        copy.wait()
    shares = lax.dot_general(
        q_sum[...], k_sum[...], (((1,), (1,)), ((), ())), precision=lax.Precision.HIGHEST, preferred_element_type=F32
    )
    part[...] = (shares * PRICE).reshape(N_HEADS, 8, 128)
    reduces = []
    for d in range(1, N_HEADS):
        to = lax.rem(z + d, N_HEADS)
        reduces.append(remote(part.at[to], part_in.at[z], red_send.at[d], red_recv.at[d], floor(d)))
    for copy in reduces:
        copy.start()
    part_in[z] = part[z]
    for copy in reduces:
        copy.wait()
    cost[z, yc, x] = jnp.sum(part_in[...], axis=0)
    tiles = []
    for d in (1, 2, 3):
        tile = cost.at[z, yc, x]
        tiles.append(remote(tile, tile, tile_send.at[d], tile_recv.at[d], device(d, 0, 0)))
    for copy in tiles:
        copy.start()
    for copy in tiles:
        copy.wait()
    tiles = []
    for r in range(1, 8):
        strip = cost.at[z, yc]
        tiles.append(remote(strip, strip, tile_send.at[3 + r], tile_recv.at[3 + r], device(0, r // 2, r % 2)))
    for copy in tiles:
        copy.start()
    for copy in tiles:
        copy.wait()
    tiles = []
    for d in range(1, N_HEADS):
        layer = cost.at[z]
        tiles.append(remote(layer, layer, tile_send.at[10 + d], tile_recv.at[10 + d], floor(d)))
    for copy in tiles:
        copy.start()

    for d in (2, 1, 3):
        def pass_k(u, d=d):
            t = rest_k(d)(u)
            first_k(t, False).wait_recv()
            second_k(t, False).start()

        def pass_v(u, d=d):
            t = rest_v(d)(u)
            first_v(t, False).wait_recv()
            second_v(t, False).start()

        each(7, pass_k)
        each(7, pass_v)
    each(7, start_near_k)
    each(7, start_near_v)

    for copy in tiles:
        copy.wait()

    col_pot[...] = jnp.zeros_like(col_pot)

    def refit(repeat, carry):
        inverse = 1.0 / soft[repeat]

        def rows(k, carry):
            scaled = cost[k] * inverse + col_pot[...][None]
            top = jnp.max(jnp.max(scaled, axis=1), axis=-1, keepdims=True)
            total = jnp.sum(jnp.sum(jnp.exp(scaled - top[:, None]), axis=1), axis=-1, keepdims=True)
            row_pot[k] = jnp.broadcast_to(-(top + jnp.log(total)), (8, 8, 128))
            return carry

        lax.fori_loop(0, N_HEADS, rows, 0)

        def tops(k, top):
            scaled = cost[k] * inverse + row_pot[k][:, None]
            return jnp.maximum(top, jnp.max(scaled, axis=0))

        top = lax.fori_loop(0, N_HEADS, tops, jnp.full((4, 8, 128), -jnp.inf, F32))
        top = jnp.broadcast_to(jnp.max(top, axis=1, keepdims=True), (4, 8, 128))

        def totals(k, total):
            scaled = cost[k] * inverse + row_pot[k][:, None]
            return total + jnp.sum(jnp.exp(scaled - top[None]), axis=0)

        total = lax.fori_loop(0, N_HEADS, totals, jnp.zeros((4, 8, 128), F32))
        total = jnp.broadcast_to(jnp.sum(total, axis=1, keepdims=True), (4, 8, 128))
        col_pot[...] = -(top + jnp.log(total))
        return carry

    lax.fori_loop(0, REFIT_REPEATS, refit, 0)
    inverse = 1.0 / soft[REFIT_REPEATS - 1]
    for half in range(2):
        k = x * 2 + half
        coupling = cost[k, yc] * inverse + row_pot[k, yc][None] + col_pot[...] + math.log(ALL_BLOCKS)
        for column in range(4):
            mine[half * 8 : half * 8 + 8, column * 128 : column * 128 + 128] = coupling[column]

    columns = lax.broadcasted_iota(jnp.int32, (BLOCKS_DEV, ALL_BLOCKS), 1)
    queries = lax.broadcasted_iota(jnp.int32, (BLOCKS_DEV, ALL_BLOCKS), 0)

    def attend(t):
        dx, dy, dc = split_slot(t)
        source = place(4 - dx, 4 - dy, dc)
        index, column = route[QUERY, source], route[COLUMN, source]
        entry = jnp.logical_and(columns == column, queries == index)
        bias = jnp.sum(jnp.sum(jnp.where(entry, mine[...], 0.0), axis=0, keepdims=True), axis=1, keepdims=True)
        for h in range(GROUP_HEADS):
            lanes = slice(h * HEAD_DIM, (h + 1) * HEAD_DIM)
            q = q_ref[index, :, lanes]
            turned = (((1,), (1,)), ((), ()))
            near = lax.dot_general(kv_ref[0, index, :, lanes], q, turned, preferred_element_type=F32) * SCALE
            far = lax.dot_general(fin_k[t, :, lanes], q, turned, preferred_element_type=F32) * SCALE + bias
            joint = jnp.maximum(jnp.max(near, axis=0, keepdims=True), jnp.max(far, axis=0, keepdims=True))
            near_expo, far_expo = jnp.exp(near - joint), jnp.exp(far - joint)
            total = jnp.sum(near_expo, axis=0, keepdims=True) + jnp.sum(far_expo, axis=0, keepdims=True)
            moment = jnp.sum(near_expo * near + far_expo * far, axis=0, keepdims=True)
            share = 1.0 / total
            down = (((0,), (0,)), ((), ()))
            mixed = lax.dot_general(
                (near_expo * share).astype(jnp.bfloat16), kv_ref[1, index, :, lanes], down, preferred_element_type=F32
            ) + lax.dot_general(
                (far_expo * share).astype(jnp.bfloat16), fin_v[t, :, lanes], down, preferred_element_type=F32
            )
            out_slot[source, :, lanes] = mixed.astype(jnp.bfloat16)
            ent_slot[source, h : h + 1, :] = jnp.log(total) + joint - moment * share

    attend(0)

    def arrived(t):
        second_k(t, True).wait_recv()
        second_v(t, True).wait_recv()
        attend(t)

    each(N_SEQ - 1, lambda u: arrived(u + 1))

    lane = lax.broadcasted_iota(jnp.int32, (GROUP_HEADS, 128), 1)
    entropy = jnp.zeros((GROUP_HEADS, 128), F32)
    for i in range(BLOCKS_DEV):
        source = route[OWNER, i]
        att_ref[i] = out_slot[source]
        mean = jnp.sum(ent_slot[source], axis=1, keepdims=True) * (1.0 / BLOCK)
        entropy = jnp.where(lane == i, mean, entropy)
    ent_ref[...] = entropy[:, :BLOCKS_DEV]

    for d in (1, 2, 3):
        each(8, lambda u, d=d: first_k(d * 8 + u, False).wait_send())
        each(8, lambda u, d=d: first_v((u // 2) * 8 + d * 2 + u % 2, False).wait_send())
    for d in range(4):
        each(7, lambda u, d=d: second_k(rest_k(d)(u), True).wait_send())
        each(7, lambda u, d=d: second_v(rest_v(d)(u), True).wait_send())


def routes(chart):
    seq = lax.axis_index("seq")
    table = chart.reshape(N_SEQ, BLOCKS_DEV)
    wanted = jnp.sum(jnp.where(table // BLOCKS_DEV == seq, table % BLOCKS_DEV, 0), axis=1)
    own = lax.dynamic_index_in_dim(table, seq, 0, keepdims=False)
    owner = own // BLOCKS_DEV
    hit = jnp.arange(N_SEQ, dtype=jnp.int32)[:, None] == owner[None, :]
    query = jnp.sum(jnp.where(hit, jnp.arange(BLOCKS_DEV, dtype=jnp.int32)[None, :], 0), axis=1)
    column = jnp.sum(jnp.where(hit, own[None, :], 0), axis=1)
    return jnp.stack([wanted, query, column, jnp.concatenate([owner, owner])])


def on_device(queries, pile, softness, chart):
    slots = pltpu.VMEM((N_SEQ, BLOCK, WIDTH), jnp.bfloat16)
    dma = pltpu.SemaphoreType.DMA
    smem = pl.BlockSpec(memory_space=pltpu.SMEM)
    vmem = pl.BlockSpec(memory_space=pltpu.VMEM)
    attended, entropy = pl.pallas_call(
        kernel,
        out_shape=(
            jax.ShapeDtypeStruct((BLOCKS_DEV, BLOCK, WIDTH), jnp.bfloat16),
            jax.ShapeDtypeStruct((GROUP_HEADS, BLOCKS_DEV), F32),
        ),
        in_specs=[smem, smem, vmem, vmem],
        out_specs=(vmem, vmem),
        scratch_shapes=[
            slots, slots, slots, slots, slots, slots, slots,
            pltpu.VMEM((N_SEQ, GROUP_HEADS, 128), F32),
            pltpu.VMEM((64, WIDTH), F32),
            pltpu.VMEM((128, WIDTH), F32),
            pltpu.VMEM((N_HEADS, 8, 128), F32),
            pltpu.VMEM((N_HEADS, 8, 128), F32),
            pltpu.VMEM((N_HEADS, 8, 4, 8, 128), F32),
            pltpu.VMEM((N_HEADS, 8, 8, 128), F32),
            pltpu.VMEM((4, 8, 128), F32),
            pltpu.VMEM((BLOCKS_DEV, ALL_BLOCKS), F32),
            dma((11,)), dma((11,)), dma((8,)), dma((8,)), dma((18,)), dma((18,)),
            dma((N_SEQ,)), dma((N_SEQ,)), dma((N_SEQ,)), dma((N_SEQ,)),
            dma((N_SEQ,)), dma((N_SEQ,)), dma((N_SEQ,)), dma((N_SEQ,)),
        ],
        compiler_params=pltpu.CompilerParams(
            collective_id=0, has_side_effects=True, vmem_limit_bytes=60 * 1024 * 1024
        ),
        name="sparse_attention",
    )(
        routes(chart), softness, queries.reshape(BLOCKS_DEV, BLOCK, WIDTH), pile.reshape(2, BLOCKS_DEV, BLOCK, WIDTH)
    )
    return attended.reshape(queries.shape), entropy


def solution(mesh):
    in_specs = (P("seq", "heads"), P(None, "seq", "heads"), P(), P("heads", None))
    out_specs = (P("seq", "heads"), P("heads", "seq"))
    return jax.shard_map(
        on_device, mesh=mesh, in_specs=in_specs, out_specs=out_specs, check_vma=False
    )
```

```python
import math

import jax
import jax.numpy as jnp
from jax import lax
from jax.experimental import pallas as pl
from jax.experimental.pallas import tpu as pltpu
from jax.sharding import PartitionSpec as P

HEADS = 32
HEAD_DIM = 128
BLOCK = 128
GROUP_HEADS = 4
REFIT_REPEATS = 8
WIDTH = GROUP_HEADS * HEAD_DIM
BLOCKS_DEV = 16
N_SEQ = 32
N_HEADS = 8
ALL_BLOCKS = BLOCKS_DEV * N_SEQ
MESH = pl.DeviceIdType.MESH
F32 = jnp.float32
PRICE = 1.0 / (BLOCK * math.sqrt(HEAD_DIM * HEADS))
SCALE = HEAD_DIM ** (-0.5)
LOG2E = math.log2(math.e)
WANTED, QUERY, PARTNER, OWNER = range(4)


def split_slot(t):
    return t // 8, (t // 2) % 4, t % 2


def kernel(
    route, soft, q_hbm, kv_hbm, att_ref, ent_ref, q_ref, kv_ref, near_expo, near_stat,
    pack_k, pack_v, mid_k, mid_v, fin_k, fin_v, out_slot, ent_slot,
    q_sum, k_sum, part, part_in, cost, row_pot, col_pot, mine,
    load_sem, sum_send, sum_recv, red_send, red_recv, tile_send, tile_recv,
    first_k_send, first_v_send, mid_k_recv, mid_v_recv,
    second_k_send, second_v_send, fin_k_recv, fin_v_recv,
):
    seq = lax.axis_index("seq")
    z = lax.axis_index("heads")
    x, y, c = seq // 8, (seq // 2) % 4, seq % 2
    yc = seq % 8

    def place(dx, dy, dc):
        return lax.rem(x + dx, 4) * 8 + lax.rem(y + dy, 4) * 2 + lax.rem(c + dc, 2)

    def device(dx, dy, dc):
        return (z, place(dx, dy, dc))

    def floor(dz):
        return (lax.rem(z + dz, N_HEADS), seq)

    def remote(src, dst, send, recv, to):
        return pltpu.make_async_remote_copy(
            src_ref=src, dst_ref=dst, send_sem=send, recv_sem=recv, device_id=to, device_id_type=MESH
        )

    load_k = pltpu.make_async_copy(kv_hbm.at[0], kv_ref.at[0], load_sem.at[0])
    load_q = pltpu.make_async_copy(q_hbm, q_ref, load_sem.at[1])
    load_v = pltpu.make_async_copy(kv_hbm.at[1], kv_ref.at[1], load_sem.at[2])
    load_k.start()
    load_q.start()
    load_v.start()
    barrier = pltpu.get_barrier_semaphore()
    peers = [device(d, 0, e) for d in (1, 2, 3) for e in (0, 1)]
    peers += [device(0, d, e) for d in (1, 2, 3) for e in (0, 1)]
    peers += [device(0, 0, 1)] + [floor(d) for d in range(1, N_HEADS)]
    for peer in peers:
        pl.semaphore_signal(barrier, inc=1, device_id=peer, device_id_type=MESH)

    q_rows = pl.ds(pl.multiple_of(x * BLOCKS_DEV, BLOCKS_DEV), BLOCKS_DEV)
    k_rows = pl.ds(pl.multiple_of(yc * BLOCKS_DEV, BLOCKS_DEV), BLOCKS_DEV)
    load_k.wait()
    k_sum[k_rows, :] = jnp.sum(kv_ref[0].astype(F32), axis=1)
    load_q.wait()
    q_sum[q_rows, :] = jnp.sum(q_ref[...].astype(F32), axis=1)

    pl.semaphore_wait(barrier, len(peers))

    sums = []
    for d in (1, 2, 3):
        sums.append(remote(q_sum.at[q_rows], q_sum.at[q_rows], sum_send.at[d], sum_recv.at[d], device(d, 0, 0)))
    for r in range(1, 8):
        sums.append(
            remote(k_sum.at[k_rows], k_sum.at[k_rows], sum_send.at[3 + r], sum_recv.at[3 + r], device(0, r // 2, r % 2))
        )
    for copy in sums:
        copy.start()

    def first_k(t, final):
        dst, recv = (fin_k, fin_k_recv) if final else (mid_k, mid_k_recv)
        return remote(pack_k.at[t], dst.at[t], first_k_send.at[t], recv.at[t], device(t // 8, 0, 0))

    def first_v(t, final):
        dst, recv = (fin_v, fin_v_recv) if final else (mid_v, mid_v_recv)
        return remote(pack_v.at[t], dst.at[t], first_v_send.at[t], recv.at[t], device(0, (t // 2) % 4, 0))

    def second_k(t, direct):
        src = pack_k if direct else mid_k
        _, dy, dc = split_slot(t)
        return remote(src.at[t], fin_k.at[t], second_k_send.at[t], fin_k_recv.at[t], device(0, dy, dc))

    def second_v(t, direct):
        src = pack_v if direct else mid_v
        dx, _, dc = split_slot(t)
        return remote(src.at[t], fin_v.at[t], second_v_send.at[t], fin_v_recv.at[t], device(dx, 0, dc))

    def is_final_k(t):
        return t % 8 == 0

    def is_final_v(t):
        return t // 8 == 0 and t % 2 == 0

    def nth_slot(u):
        j = (u // 2) % 4
        return ((j + 1) % 4) * 8 + ((j + u // 8 + 1) % 4) * 2 + u % 2

    order = [nth_slot(u) for u in range(N_SEQ)]

    def fill_k(t, into):
        into[t] = kv_ref[0, route[WANTED, place(*split_slot(t))]]

    def fill_v(t, into):
        into[t] = kv_ref[1, route[WANTED, place(*split_slot(t))]]

    load_v.wait()
    for t in order:
        dx, dy, dc = split_slot(t)
        fill_k(t, pack_k if t else fin_k)
        if dx:
            first_k(t, is_final_k(t)).start()
        fill_v(t, pack_v if t else fin_v)
        if dy:
            first_v(t, is_final_v(t)).start()

    turned = (((1,), (1,)), ((), ()))

    heads = [slice(h * HEAD_DIM, (h + 1) * HEAD_DIM) for h in range(GROUP_HEADS)]

    def softmax_part(keys, queries):
        scores = [lax.dot_general(k, q, turned, preferred_element_type=F32) for k, q in zip(keys, queries)]
        tops = [jnp.max(score, axis=0, keepdims=True) for score in scores]
        expos = [jnp.exp2((score - top) * (SCALE * LOG2E)) for score, top in zip(scores, tops)]
        totals = [jnp.sum(expo, axis=0, keepdims=True) for expo in expos]
        moments = [jnp.sum(expo * score, axis=0, keepdims=True) for expo, score in zip(expos, scores)]
        stack = lambda rows: jnp.concatenate(rows, axis=0)
        return expos, stack(tops) * SCALE, stack(totals), stack(moments) * SCALE

    def near_part(i):
        expos, top, total, moment = softmax_part(
            [kv_ref[0, i, :, lanes] for lanes in heads], [q_ref[i, :, lanes] for lanes in heads]
        )
        for h in range(GROUP_HEADS):
            near_expo[i, h] = expos[h]
        near_stat[i, 0] = top
        near_stat[i, 1] = total
        near_stat[i, 2] = moment

    def near_parts(first):
        def step(u, carry):
            near_part(first + u)
            return carry

        lax.fori_loop(0, 4, step, 0)

    for copy in sums:
        copy.wait()
    shares = lax.dot_general(
        q_sum[...], k_sum[...], (((1,), (1,)), ((), ())), precision=lax.Precision.HIGHEST, preferred_element_type=F32
    )
    part[...] = (shares * PRICE).reshape(N_HEADS, 8, 128)
    reduces = []
    for d in range(1, N_HEADS):
        to = lax.rem(z + d, N_HEADS)
        reduces.append(remote(part.at[to], part_in.at[z], red_send.at[d], red_recv.at[d], floor(d)))
    for copy in reduces:
        copy.start()
    part_in[z] = part[z]
    near_parts(0)
    for copy in reduces:
        copy.wait()
    cost[z, yc, x] = jnp.sum(part_in[...], axis=0)
    tiles = []
    for d in (1, 2, 3):
        tile = cost.at[z, yc, x]
        tiles.append(remote(tile, tile, tile_send.at[d], tile_recv.at[d], device(d, 0, 0)))
    for copy in tiles:
        copy.start()
    near_parts(4)
    for copy in tiles:
        copy.wait()
    tiles = []
    for r in range(1, 8):
        strip = cost.at[z, yc]
        tiles.append(remote(strip, strip, tile_send.at[3 + r], tile_recv.at[3 + r], device(0, r // 2, r % 2)))
    for copy in tiles:
        copy.start()
    near_parts(8)
    for copy in tiles:
        copy.wait()
    tiles = []
    for d in range(1, N_HEADS):
        layer = cost.at[z]
        tiles.append(remote(layer, layer, tile_send.at[10 + d], tile_recv.at[10 + d], floor(d)))
    for copy in tiles:
        copy.start()

    near_parts(12)
    for t in order:
        dx, dy, dc = split_slot(t)
        if dx and not is_final_k(t):
            first_k(t, False).wait_recv()
        if not is_final_k(t):
            second_k(t, dx == 0).start()
        if dy and not is_final_v(t):
            first_v(t, False).wait_recv()
        if not is_final_v(t):
            second_v(t, dy == 0).start()

    for copy in tiles:
        copy.wait()

    col_pot[...] = jnp.zeros_like(col_pot)

    def refit(repeat, carry):
        inverse = LOG2E / soft[repeat]

        def rows(k, carry):
            scaled = cost[k] * inverse + col_pot[...][None]
            top = jnp.max(jnp.max(scaled, axis=1), axis=-1, keepdims=True)
            total = jnp.sum(jnp.sum(jnp.exp2(scaled - top[:, None]), axis=1), axis=-1, keepdims=True)
            row_pot[k] = jnp.broadcast_to(-(top + jnp.log2(total)), (8, 8, 128))
            return carry

        lax.fori_loop(0, N_HEADS, rows, 0, unroll=4)

        def tops(k, top):
            scaled = cost[k] * inverse + row_pot[k][:, None]
            return jnp.maximum(top, jnp.max(scaled, axis=0))

        top = lax.fori_loop(0, N_HEADS, tops, jnp.full((4, 8, 128), -jnp.inf, F32), unroll=2)
        top = jnp.broadcast_to(jnp.max(top, axis=1, keepdims=True), (4, 8, 128))

        def totals(k, total):
            scaled = cost[k] * inverse + row_pot[k][:, None]
            return total + jnp.sum(jnp.exp2(scaled - top[None]), axis=0)

        total = lax.fori_loop(0, N_HEADS, totals, jnp.zeros((4, 8, 128), F32), unroll=2)
        total = jnp.broadcast_to(jnp.sum(total, axis=1, keepdims=True), (4, 8, 128))
        col_pot[...] = -(top + jnp.log2(total))
        return carry

    lax.fori_loop(0, REFIT_REPEATS, refit, 0)
    inverse = LOG2E / soft[REFIT_REPEATS - 1]
    for half in range(2):
        k = x * 2 + half
        coupling = (cost[k, yc] * inverse + row_pot[k, yc][None] + col_pot[...]) * math.log(2.0) + math.log(ALL_BLOCKS)
        for column in range(4):
            mine[half * 8 : half * 8 + 8, column * 128 : column * 128 + 128] = coupling[column]

    queries = lax.broadcasted_iota(jnp.int32, (BLOCKS_DEV, 128), 0)
    partner = jnp.zeros((BLOCKS_DEV, 128), jnp.int32)
    for i in range(BLOCKS_DEV):
        partner = jnp.where(queries == i, route[PARTNER, i], partner)
    partner = jnp.concatenate([partner] * 4, axis=1)
    columns = lax.broadcasted_iota(jnp.int32, (BLOCKS_DEV, ALL_BLOCKS), 1)
    biases = jnp.sum(jnp.where(columns == partner, mine[...], 0.0), axis=1, keepdims=True)
    for i in range(BLOCKS_DEV):
        near_stat[i, 3] = jnp.broadcast_to(biases[i : i + 1], (GROUP_HEADS, 128))

    def attend(t):
        dx, dy, dc = split_slot(t)
        source = place(4 - dx, 4 - dy, dc)
        index = route[QUERY, source]
        expos, top, total, moment = softmax_part(
            [fin_k[t, :, lanes] for lanes in heads], [q_ref[index, :, lanes] for lanes in heads]
        )
        near_top, near_total, near_moment = near_stat[index, 0], near_stat[index, 1], near_stat[index, 2]
        bias = near_stat[index, 3]
        shifted = top + bias
        joint = jnp.maximum(near_top, shifted)
        near_weight, weight = jnp.exp(near_top - joint), jnp.exp(shifted - joint)
        denominator = near_total * near_weight + total * weight
        inverse = 1.0 / denominator
        near_weight, weight = near_weight * inverse, weight * inverse
        ent_slot[source] = (
            jnp.log(denominator) + joint - (near_moment * near_weight + (moment + bias * total) * weight)
        )
        shares = [
            jnp.concatenate(
                [near_expo[index, h] * near_weight[h : h + 1], expos[h] * weight[h : h + 1]], axis=0
            ).astype(jnp.bfloat16)
            for h in range(GROUP_HEADS)
        ]
        values = [
            jnp.concatenate([kv_ref[1, index, :, lanes], fin_v[t, :, lanes]], axis=0) for lanes in heads
        ]
        mixed = [
            lax.dot_general(p, v, (((0,), (0,)), ((), ())), preferred_element_type=F32) for p, v in zip(shares, values)
        ]
        for h, lanes in enumerate(heads):
            out_slot[source, :, lanes] = mixed[h].astype(jnp.bfloat16)

    def arrived(u, carry):
        t = nth_slot(u)

        @pl.when(t != 0)
        def _():
            second_k(t, True).wait_recv()
            second_v(t, True).wait_recv()

        attend(t)
        return carry

    lax.fori_loop(0, N_SEQ, arrived, 0)

    lane = lax.broadcasted_iota(jnp.int32, (GROUP_HEADS, 128), 1)
    entropy = jnp.zeros((GROUP_HEADS, 128), F32)
    for i in range(BLOCKS_DEV):
        source = route[OWNER, i]
        att_ref[i] = out_slot[source]
        mean = jnp.sum(ent_slot[source], axis=1, keepdims=True) * (1.0 / BLOCK)
        entropy = jnp.where(lane == i, mean, entropy)
    ent_ref[...] = entropy[:, :BLOCKS_DEV]

    for t in order:
        dx, dy, dc = split_slot(t)
        if dx:
            first_k(t, False).wait_send()
        if dy:
            first_v(t, False).wait_send()
        if not is_final_k(t):
            second_k(t, True).wait_send()
        if not is_final_v(t):
            second_v(t, True).wait_send()


def routes(chart):
    seq = lax.axis_index("seq")
    table = chart.reshape(N_SEQ, BLOCKS_DEV)
    wanted = jnp.sum(jnp.where(table // BLOCKS_DEV == seq, table % BLOCKS_DEV, 0), axis=1)
    own = lax.dynamic_index_in_dim(table, seq, 0, keepdims=False)
    owner = own // BLOCKS_DEV
    hit = jnp.arange(N_SEQ, dtype=jnp.int32)[:, None] == owner[None, :]
    query = jnp.sum(jnp.where(hit, jnp.arange(BLOCKS_DEV, dtype=jnp.int32)[None, :], 0), axis=1)
    return jnp.stack([wanted, query, jnp.concatenate([own, own]), jnp.concatenate([owner, owner])])


def on_device(queries, pile, softness, chart):
    slots = pltpu.VMEM((N_SEQ, BLOCK, WIDTH), jnp.bfloat16)
    dma = pltpu.SemaphoreType.DMA
    smem = pl.BlockSpec(memory_space=pltpu.SMEM)
    vmem = pl.BlockSpec(memory_space=pltpu.VMEM)
    attended, entropy = pl.pallas_call(
        kernel,
        out_shape=(
            jax.ShapeDtypeStruct((BLOCKS_DEV, BLOCK, WIDTH), jnp.bfloat16),
            jax.ShapeDtypeStruct((GROUP_HEADS, BLOCKS_DEV), F32),
        ),
        in_specs=[smem, smem, pl.BlockSpec(memory_space=pl.ANY), pl.BlockSpec(memory_space=pl.ANY)],
        out_specs=(vmem, vmem),
        scratch_shapes=[
            pltpu.VMEM((BLOCKS_DEV, BLOCK, WIDTH), jnp.bfloat16),
            pltpu.VMEM((2, BLOCKS_DEV, BLOCK, WIDTH), jnp.bfloat16),
            pltpu.VMEM((BLOCKS_DEV, GROUP_HEADS, BLOCK, BLOCK), F32),
            pltpu.VMEM((BLOCKS_DEV, 4, GROUP_HEADS, BLOCK), F32),
            slots, slots, slots, slots, slots, slots, slots,
            pltpu.VMEM((N_SEQ, GROUP_HEADS, 128), F32),
            pltpu.VMEM((64, WIDTH), F32),
            pltpu.VMEM((128, WIDTH), F32),
            pltpu.VMEM((N_HEADS, 8, 128), F32),
            pltpu.VMEM((N_HEADS, 8, 128), F32),
            pltpu.VMEM((N_HEADS, 8, 4, 8, 128), F32),
            pltpu.VMEM((N_HEADS, 8, 8, 128), F32),
            pltpu.VMEM((4, 8, 128), F32),
            pltpu.VMEM((BLOCKS_DEV, ALL_BLOCKS), F32),
            dma((3,)), dma((11,)), dma((11,)), dma((8,)), dma((8,)), dma((18,)), dma((18,)),
            dma((N_SEQ,)), dma((N_SEQ,)), dma((N_SEQ,)), dma((N_SEQ,)),
            dma((N_SEQ,)), dma((N_SEQ,)), dma((N_SEQ,)), dma((N_SEQ,)),
        ],
        compiler_params=pltpu.CompilerParams(
            collective_id=0, has_side_effects=True, vmem_limit_bytes=60 * 1024 * 1024
        ),
        name="sparse_attention",
    )(
        routes(chart), softness, queries.reshape(BLOCKS_DEV, BLOCK, WIDTH), pile.reshape(2, BLOCKS_DEV, BLOCK, WIDTH)
    )
    return attended.reshape(queries.shape), entropy


def solution(mesh):
    in_specs = (P("seq", "heads"), P(None, "seq", "heads"), P(), P("heads", None))
    out_specs = (P("seq", "heads"), P("heads", "seq"))
    return jax.shard_map(
        on_device, mesh=mesh, in_specs=in_specs, out_specs=out_specs, check_vma=False
    )
```

```python
import math

import jax
import jax.numpy as jnp
from jax import lax
from jax.experimental import pallas as pl
from jax.experimental.pallas import tpu as pltpu
from jax.sharding import PartitionSpec as P

HEADS = 32
HEAD_DIM = 128
BLOCK = 128
GROUP_HEADS = 4
REFIT_REPEATS = 8
WIDTH = GROUP_HEADS * HEAD_DIM
BLOCKS_DEV = 16
N_SEQ = 32
N_HEADS = 8
ALL_BLOCKS = BLOCKS_DEV * N_SEQ
MESH = pl.DeviceIdType.MESH
F32 = jnp.float32
PRICE = 1.0 / (BLOCK * math.sqrt(HEAD_DIM * HEADS))
SCALE = HEAD_DIM ** (-0.5)
LOG2E = math.log2(math.e)


def split_slot(t):
    return t // 8, (t // 2) % 4, t % 2


def kernel(
    chart, soft, q_hbm, kv_hbm, att_hbm, ent_slot, q_ref, k_ref, v_ref, near_expo, near_stat,
    pack_k, pack_v, mid_k, mid_v, fin_k, fin_v, out_slot,
    q_sum, k_sum, part, part_in, cost, row_pot, col_pot, mine,
    load_sem, out_sem, sum_send, sum_recv, red_send, red_recv, tile_send, tile_recv,
    first_k_send, first_v_send, mid_k_recv, mid_v_recv,
    second_k_send, second_v_send, fin_k_recv, fin_v_recv,
):
    seq = lax.axis_index("seq")
    z = lax.axis_index("heads")
    x, y, c = seq // 8, (seq // 2) % 4, seq % 2
    yc = seq % 8

    def place(dx, dy, dc):
        return lax.rem(x + dx, 4) * 8 + lax.rem(y + dy, 4) * 2 + lax.rem(c + dc, 2)

    def device(dx, dy, dc):
        return (z, place(dx, dy, dc))

    def floor(dz):
        return (lax.rem(z + dz, N_HEADS), seq)

    def remote(src, dst, send, recv, to):
        return pltpu.make_async_remote_copy(
            src_ref=src, dst_ref=dst, send_sem=send, recv_sem=recv, device_id=to, device_id_type=MESH
        )

    load_k = pltpu.make_async_copy(kv_hbm.at[0], k_ref, load_sem.at[0])
    load_q = pltpu.make_async_copy(q_hbm, q_ref, load_sem.at[1])
    load_v = pltpu.make_async_copy(kv_hbm.at[1], v_ref, load_sem.at[2])
    load_k.start()
    load_v.start()
    load_q.start()
    barrier = pltpu.get_barrier_semaphore()
    peers = [device(d, 0, e) for d in (1, 2, 3) for e in (0, 1)]
    peers += [device(0, d, e) for d in (1, 2, 3) for e in (0, 1)]
    peers += [device(0, 0, 1)] + [floor(d) for d in range(1, N_HEADS)]
    for peer in peers:
        pl.semaphore_signal(barrier, inc=1, device_id=peer, device_id_type=MESH)

    def first_k(t, final):
        dst, recv = (fin_k, fin_k_recv) if final else (mid_k, mid_k_recv)
        return remote(pack_k.at[t], dst.at[t], first_k_send.at[t], recv.at[t], device(t // 8, 0, 0))

    def first_v(t, final):
        dst, recv = (fin_v, fin_v_recv) if final else (mid_v, mid_v_recv)
        return remote(pack_v.at[t], dst.at[t], first_v_send.at[t], recv.at[t], device(0, (t // 2) % 4, 0))

    def second_k(t, direct):
        src = pack_k if direct else mid_k
        _, dy, dc = split_slot(t)
        return remote(src.at[t], fin_k.at[t], second_k_send.at[t], fin_k_recv.at[t], device(0, dy, dc))

    def second_v(t, direct):
        src = pack_v if direct else mid_v
        dx, _, dc = split_slot(t)
        return remote(src.at[t], fin_v.at[t], second_v_send.at[t], fin_v_recv.at[t], device(dx, 0, dc))

    def is_final_k(t):
        return t % 8 == 0

    def is_final_v(t):
        return t // 8 == 0 and t % 2 == 0

    def nth_slot(u):
        j = (u // 2) % 4
        return ((j + 1) % 4) * 8 + ((j + u // 8 + 1) % 4) * 2 + u % 2

    order = [nth_slot(u) for u in range(N_SEQ)]

    def wanted(t):
        first = place(*split_slot(t)) * BLOCKS_DEV
        index = jnp.int32(0)
        for i in range(BLOCKS_DEV):
            entry = chart[0, first + i]
            index = jnp.maximum(index, jnp.where(entry >> 4 == seq, entry & (BLOCKS_DEV - 1), 0))
        return index

    def send_k(t, index):
        into = pack_k if t else fin_k
        into[t] = k_ref[index]
        if t // 8:
            first_k(t, is_final_k(t)).start()

    def send_v(t, index):
        into = pack_v if t else fin_v
        into[t] = v_ref[index]
        if (t // 2) % 4:
            first_v(t, is_final_v(t)).start()

    def send_slots(slots):
        for t in slots:
            index = wanted(t)
            send_k(t, index)
            send_v(t, index)

    load_k.wait()
    pl.semaphore_wait(barrier, len(peers))
    early = [(t, wanted(t)) for t in order[:4]]
    for t, index in early:
        send_k(t, index)
    load_v.wait()
    for t, index in early:
        send_v(t, index)

    q_rows = pl.ds(pl.multiple_of(x * BLOCKS_DEV, BLOCKS_DEV), BLOCKS_DEV)
    k_rows = pl.ds(pl.multiple_of(yc * BLOCKS_DEV, BLOCKS_DEV), BLOCKS_DEV)
    k_sum[k_rows, :] = jnp.sum(k_ref[...].astype(F32), axis=1)
    load_q.wait()
    q_sum[q_rows, :] = jnp.sum(q_ref[...].astype(F32), axis=1)
    sums = []
    for d in (1, 2, 3):
        sums.append(remote(q_sum.at[q_rows], q_sum.at[q_rows], sum_send.at[d], sum_recv.at[d], device(d, 0, 0)))
    for r in range(1, 8):
        sums.append(
            remote(k_sum.at[k_rows], k_sum.at[k_rows], sum_send.at[3 + r], sum_recv.at[3 + r], device(0, r // 2, r % 2))
        )
    for copy in sums:
        copy.start()
    send_slots(order[4:12])

    def pass_slots(slots):
        for t in slots:
            dx, dy, dc = split_slot(t)
            if dx and not is_final_k(t):
                first_k(t, False).wait_recv()
            if not is_final_k(t):
                second_k(t, dx == 0).start()
            if dy and not is_final_v(t):
                first_v(t, False).wait_recv()
            if not is_final_v(t):
                second_v(t, dy == 0).start()

    turned = (((1,), (1,)), ((), ()))

    heads = [slice(h * HEAD_DIM, (h + 1) * HEAD_DIM) for h in range(GROUP_HEADS)]

    def softmax_part(keys, queries):
        scores = [lax.dot_general(k, q, turned, preferred_element_type=F32) for k, q in zip(keys, queries)]
        tops = [jnp.max(score, axis=0, keepdims=True) for score in scores]
        expos = [jnp.exp2((score - top) * (SCALE * LOG2E)) for score, top in zip(scores, tops)]
        totals = [jnp.sum(expo, axis=0, keepdims=True) for expo in expos]
        moments = [jnp.sum(expo * score, axis=0, keepdims=True) for expo, score in zip(expos, scores)]
        stack = lambda rows: jnp.concatenate(rows, axis=0)
        return expos, stack(tops) * SCALE, stack(totals), stack(moments) * SCALE

    def near_part(i):
        expos, top, total, moment = softmax_part(
            [k_ref[i, :, lanes] for lanes in heads], [q_ref[i, :, lanes] for lanes in heads]
        )
        for h in range(GROUP_HEADS):
            near_expo[i, h] = expos[h]
        near_stat[i, 0] = top
        near_stat[i, 1] = total
        near_stat[i, 2] = moment

    def near_parts(first):
        def step(u, carry):
            near_part(first + u)
            return carry

        lax.fori_loop(0, 4, step, 0)

    for copy in sums:
        copy.wait()
    shares = lax.dot_general(
        q_sum[...], k_sum[...], (((1,), (1,)), ((), ())), precision=lax.Precision.HIGHEST, preferred_element_type=F32
    )
    part[...] = (shares * PRICE).reshape(N_HEADS, 8, 128)
    reduces = []
    for d in range(1, N_HEADS):
        to = lax.rem(z + d, N_HEADS)
        reduces.append(remote(part.at[to], part_in.at[z], red_send.at[d], red_recv.at[d], floor(d)))
    for copy in reduces:
        copy.start()
    part_in[z] = part[z]
    send_slots(order[12:20])
    near_parts(0)
    for copy in reduces:
        copy.wait()
    cost[z, yc, x] = jnp.sum(part_in[...], axis=0)
    tiles = []
    for d in (1, 2, 3):
        tile = cost.at[z, yc, x]
        tiles.append(remote(tile, tile, tile_send.at[d], tile_recv.at[d], device(d, 0, 0)))
    for copy in tiles:
        copy.start()
    send_slots(order[20:])
    near_parts(4)
    for copy in tiles:
        copy.wait()
    tiles = []
    for r in range(1, 8):
        strip = cost.at[z, yc]
        tiles.append(remote(strip, strip, tile_send.at[3 + r], tile_recv.at[3 + r], device(0, r // 2, r % 2)))
    for copy in tiles:
        copy.start()
    pass_slots(order[:8])
    near_parts(8)
    for copy in tiles:
        copy.wait()
    half_layer = pl.ds(c * 4, 4)
    tiles = []
    for d in range(1, N_HEADS):
        layer = cost.at[z, half_layer]
        tiles.append(remote(layer, layer, tile_send.at[10 + d], tile_recv.at[10 + d], floor(d)))
    for copy in tiles:
        copy.start()

    near_parts(12)
    pass_slots(order[8:20])
    handed = []
    for d in range(1, N_HEADS):
        tiles[d - 1].wait()
        layer = cost.at[lax.rem(z + N_HEADS - d, N_HEADS), half_layer]
        copy = remote(layer, layer, tile_send.at[17 + d], tile_recv.at[17 + d], device(0, 0, 1))
        copy.start()
        handed.append(copy)
    pass_slots(order[20:])
    for copy in handed:
        copy.wait()

    col_pot[...] = jnp.zeros_like(col_pot)

    def refit(repeat, carry):
        inverse = LOG2E / soft[repeat]

        def rows(k, carry):
            scaled = cost[k] * inverse + col_pot[...][None]
            top = jnp.max(jnp.max(scaled, axis=1), axis=-1, keepdims=True)
            total = jnp.sum(jnp.sum(jnp.exp2(scaled - top[:, None]), axis=1), axis=-1, keepdims=True)
            row_pot[k] = jnp.broadcast_to(-(top + jnp.log2(total)), (8, 8, 128))
            return carry

        lax.fori_loop(0, N_HEADS, rows, 0, unroll=4)

        def tops(k, top):
            scaled = cost[k] * inverse + row_pot[k][:, None]
            return jnp.maximum(top, jnp.max(scaled, axis=0))

        top = lax.fori_loop(0, N_HEADS, tops, jnp.full((4, 8, 128), -jnp.inf, F32), unroll=2)
        top = jnp.broadcast_to(jnp.max(top, axis=1, keepdims=True), (4, 8, 128))

        def totals(k, total):
            scaled = cost[k] * inverse + row_pot[k][:, None]
            return total + jnp.sum(jnp.exp2(scaled - top[None]), axis=0)

        total = lax.fori_loop(0, N_HEADS, totals, jnp.zeros((4, 8, 128), F32), unroll=2)
        total = jnp.broadcast_to(jnp.sum(total, axis=1, keepdims=True), (4, 8, 128))
        col_pot[...] = -(top + jnp.log2(total))
        return carry

    lax.fori_loop(0, REFIT_REPEATS, refit, 0)
    inverse = LOG2E / soft[REFIT_REPEATS - 1]
    for half in range(2):
        k = x * 2 + half
        coupling = (cost[k, yc] * inverse + row_pot[k, yc][None] + col_pot[...]) * math.log(2.0) + math.log(ALL_BLOCKS)
        for column in range(4):
            mine[half * 8 : half * 8 + 8, column * 128 : column * 128 + 128] = coupling[column]

    queries = lax.broadcasted_iota(jnp.int32, (BLOCKS_DEV, 128), 0)
    partner = jnp.zeros((BLOCKS_DEV, 128), jnp.int32)
    for i in range(BLOCKS_DEV):
        partner = jnp.where(queries == i, chart[0, seq * BLOCKS_DEV + i], partner)
    partner = jnp.concatenate([partner] * 4, axis=1)
    columns = lax.broadcasted_iota(jnp.int32, (BLOCKS_DEV, ALL_BLOCKS), 1)
    biases = jnp.sum(jnp.where(columns == partner, mine[...], 0.0), axis=1, keepdims=True)
    for i in range(BLOCKS_DEV):
        near_stat[i, 3] = jnp.broadcast_to(biases[i : i + 1], (GROUP_HEADS, 128))

    def store(source):
        return pltpu.make_async_copy(out_slot.at[source], att_hbm.at[source], out_sem.at[source])

    def attend(t):
        dx, dy, dc = split_slot(t)
        source = place(4 - dx, 4 - dy, dc)
        index = jnp.int32(0)
        for i in range(BLOCKS_DEV):
            index = jnp.maximum(index, jnp.where(chart[0, seq * BLOCKS_DEV + i] >> 4 == source, i, 0))
        expos, top, total, moment = softmax_part(
            [fin_k[t, :, lanes] for lanes in heads], [q_ref[index, :, lanes] for lanes in heads]
        )
        near_top, near_total, near_moment = near_stat[index, 0], near_stat[index, 1], near_stat[index, 2]
        bias = near_stat[index, 3]
        shifted = top + bias
        joint = jnp.maximum(near_top, shifted)
        near_weight, weight = jnp.exp(near_top - joint), jnp.exp(shifted - joint)
        denominator = near_total * near_weight + total * weight
        inverse = 1.0 / denominator
        near_weight, weight = near_weight * inverse, weight * inverse
        ent_slot[source] = (
            jnp.log(denominator) + joint - (near_moment * near_weight + (moment + bias * total) * weight)
        )
        shares = [
            jnp.concatenate(
                [near_expo[index, h] * near_weight[h : h + 1], expos[h] * weight[h : h + 1]], axis=0
            ).astype(jnp.bfloat16)
            for h in range(GROUP_HEADS)
        ]
        values = [
            jnp.concatenate([v_ref[index, :, lanes], fin_v[t, :, lanes]], axis=0) for lanes in heads
        ]
        mixed = [
            lax.dot_general(p, v, (((0,), (0,)), ((), ())), preferred_element_type=F32) for p, v in zip(shares, values)
        ]
        for h, lanes in enumerate(heads):
            out_slot[source, :, lanes] = mixed[h].astype(jnp.bfloat16)
        store(source).start()

    def arrived(u, carry):
        t = nth_slot(u)

        @pl.when(t != 0)
        def _():
            second_k(t, True).wait_recv()
            second_v(t, True).wait_recv()

        attend(t)
        return carry

    lax.fori_loop(0, N_SEQ, arrived, 0)

    def stored(source, carry):
        store(source).wait()
        return carry

    lax.fori_loop(0, N_SEQ, stored, 0)

    for t in order:
        dx, dy, dc = split_slot(t)
        if dx:
            first_k(t, False).wait_send()
        if dy:
            first_v(t, False).wait_send()
        if not is_final_k(t):
            second_k(t, True).wait_send()
        if not is_final_v(t):
            second_v(t, True).wait_send()


def in_query_order(chart, att_slot, ent_slot, att_hbm, ent_ref, held, in_sem, out_sem):
    first = lax.axis_index("seq") * BLOCKS_DEV
    sources = [chart[0, first + i] >> 4 for i in range(BLOCKS_DEV)]
    copies = [pltpu.make_async_copy(att_slot.at[source], held.at[i], in_sem.at[i]) for i, source in enumerate(sources)]
    stores = [pltpu.make_async_copy(held.at[i], att_hbm.at[i], out_sem.at[i]) for i in range(BLOCKS_DEV)]
    for copy in copies:
        copy.start()
    lane = lax.broadcasted_iota(jnp.int32, (GROUP_HEADS, 128), 1)
    entropy = jnp.zeros((GROUP_HEADS, 128), F32)
    for i, source in enumerate(sources):
        mean = jnp.sum(ent_slot[source], axis=1, keepdims=True) * (1.0 / BLOCK)
        entropy = jnp.where(lane == i, mean, entropy)
    ent_ref[...] = entropy[:, :BLOCKS_DEV]
    for copy, store in zip(copies, stores):
        copy.wait()
        store.start()
    for store in stores:
        store.wait()


def on_device(queries, pile, softness, chart):
    slots = pltpu.VMEM((N_SEQ, BLOCK, WIDTH), jnp.bfloat16)
    dma = pltpu.SemaphoreType.DMA
    smem = pl.BlockSpec(memory_space=pltpu.SMEM)
    vmem = pl.BlockSpec(memory_space=pltpu.VMEM)
    hbm = pl.BlockSpec(memory_space=pl.ANY)
    att_slot, ent_slot = pl.pallas_call(
        kernel,
        out_shape=(
            jax.ShapeDtypeStruct((N_SEQ, BLOCK, WIDTH), jnp.bfloat16),
            jax.ShapeDtypeStruct((N_SEQ, GROUP_HEADS, BLOCK), F32),
        ),
        in_specs=[smem, smem, hbm, hbm],
        out_specs=(hbm, vmem),
        scratch_shapes=[
            pltpu.VMEM((BLOCKS_DEV, BLOCK, WIDTH), jnp.bfloat16),
            pltpu.VMEM((BLOCKS_DEV, BLOCK, WIDTH), jnp.bfloat16),
            pltpu.VMEM((BLOCKS_DEV, BLOCK, WIDTH), jnp.bfloat16),
            pltpu.VMEM((BLOCKS_DEV, GROUP_HEADS, BLOCK, BLOCK), F32),
            pltpu.VMEM((BLOCKS_DEV, 4, GROUP_HEADS, BLOCK), F32),
            slots, slots, slots, slots, slots, slots, slots,
            pltpu.VMEM((64, WIDTH), F32),
            pltpu.VMEM((128, WIDTH), F32),
            pltpu.VMEM((N_HEADS, 8, 128), F32),
            pltpu.VMEM((N_HEADS, 8, 128), F32),
            pltpu.VMEM((N_HEADS, 8, 4, 8, 128), F32),
            pltpu.VMEM((N_HEADS, 8, 8, 128), F32),
            pltpu.VMEM((4, 8, 128), F32),
            pltpu.VMEM((BLOCKS_DEV, ALL_BLOCKS), F32),
            dma((3,)), dma((N_SEQ,)), dma((11,)), dma((11,)), dma((8,)), dma((8,)), dma((25,)), dma((25,)),
            dma((N_SEQ,)), dma((N_SEQ,)), dma((N_SEQ,)), dma((N_SEQ,)),
            dma((N_SEQ,)), dma((N_SEQ,)), dma((N_SEQ,)), dma((N_SEQ,)),
        ],
        compiler_params=pltpu.CompilerParams(
            collective_id=0, has_side_effects=True, vmem_limit_bytes=60 * 1024 * 1024
        ),
        name="sparse_attention",
    )(
        chart, softness, queries.reshape(BLOCKS_DEV, BLOCK, WIDTH), pile.reshape(2, BLOCKS_DEV, BLOCK, WIDTH)
    )
    attended, entropy = pl.pallas_call(
        in_query_order,
        out_shape=(
            jax.ShapeDtypeStruct((BLOCKS_DEV, BLOCK, WIDTH), jnp.bfloat16),
            jax.ShapeDtypeStruct((GROUP_HEADS, BLOCKS_DEV), F32),
        ),
        in_specs=[smem, hbm, vmem],
        out_specs=(hbm, vmem),
        scratch_shapes=[pltpu.VMEM((BLOCKS_DEV, BLOCK, WIDTH), jnp.bfloat16), dma((BLOCKS_DEV,)), dma((BLOCKS_DEV,))],
        name="query_order",
    )(chart, att_slot, ent_slot)
    return attended.reshape(queries.shape), entropy


def solution(mesh):
    in_specs = (P("seq", "heads"), P(None, "seq", "heads"), P(), P("heads", None))
    out_specs = (P("seq", "heads"), P("heads", "seq"))
    return jax.shard_map(
        on_device, mesh=mesh, in_specs=in_specs, out_specs=out_specs, check_vma=False
    )
```

```python
import math

import jax
import jax.numpy as jnp
from jax import lax
from jax.experimental import pallas as pl
from jax.experimental.pallas import tpu as pltpu
from jax.sharding import PartitionSpec as P

HEADS = 32
HEAD_DIM = 128
BLOCK = 128
GROUP_HEADS = 4
REFIT_REPEATS = 8
WIDTH = GROUP_HEADS * HEAD_DIM
BLOCKS_DEV = 16
N_SEQ = 32
N_HEADS = 8
ALL_BLOCKS = BLOCKS_DEV * N_SEQ
MESH = pl.DeviceIdType.MESH
F32 = jnp.float32
PRICE = 1.0 / (BLOCK * math.sqrt(HEAD_DIM * HEADS))
SCALE = HEAD_DIM ** (-0.5)
LOG2E = math.log2(math.e)


def split_slot(t):
    return t // 8, (t // 2) % 4, t % 2


def kernel(
    chart, soft, q_hbm, kv_hbm, att_hbm, ent_slot, q_ref, k_ref, v_ref, near_expo, near_stat,
    pack_k, pack_v, mid_k, mid_v, fin_k, fin_v, out_slot,
    q_sum, k_sum, part, part_in, cost, row_pot, col_pot, mine,
    load_sem, out_sem, sum_send, sum_recv, red_send, red_recv, tile_send, tile_recv,
    first_k_send, first_v_send, mid_k_recv, mid_v_recv,
    second_k_send, second_v_send, fin_k_recv, fin_v_recv,
):
    seq = lax.axis_index("seq")
    z = lax.axis_index("heads")
    x, y, c = seq // 8, (seq // 2) % 4, seq % 2
    strip = c * 4 + y

    def place(dx, dy, dc):
        return lax.rem(x + dx, 4) * 8 + lax.rem(y + dy, 4) * 2 + lax.rem(c + dc, 2)

    def device(dx, dy, dc):
        return (z, place(dx, dy, dc))

    def floor(dz):
        return (lax.rem(z + dz, N_HEADS), seq)

    def remote(src, dst, send, recv, to):
        return pltpu.make_async_remote_copy(
            src_ref=src, dst_ref=dst, send_sem=send, recv_sem=recv, device_id=to, device_id_type=MESH
        )

    load_k = pltpu.make_async_copy(kv_hbm.at[0], k_ref, load_sem.at[0])
    load_q = pltpu.make_async_copy(q_hbm, q_ref, load_sem.at[1])
    load_v = pltpu.make_async_copy(kv_hbm.at[1], v_ref, load_sem.at[2])
    load_k.start()
    load_v.start()
    load_q.start()
    barrier = pltpu.get_barrier_semaphore()
    peers = [device(d, 0, e) for d in (1, 2, 3) for e in (0, 1)]
    peers += [device(0, d, e) for d in (1, 2, 3) for e in (0, 1)]
    peers += [device(0, 0, 1)] + [floor(d) for d in range(1, N_HEADS)]
    for peer in peers:
        pl.semaphore_signal(barrier, inc=1, device_id=peer, device_id_type=MESH)

    def first_k(t, final):
        dst, recv = (fin_k, fin_k_recv) if final else (mid_k, mid_k_recv)
        return remote(pack_k.at[t], dst.at[t], first_k_send.at[t], recv.at[t], device(t // 8, 0, 0))

    def first_v(t, final):
        dst, recv = (fin_v, fin_v_recv) if final else (mid_v, mid_v_recv)
        return remote(pack_v.at[t], dst.at[t], first_v_send.at[t], recv.at[t], device(0, (t // 2) % 4, 0))

    def second_k(t, direct):
        src = pack_k if direct else mid_k
        _, dy, dc = split_slot(t)
        return remote(src.at[t], fin_k.at[t], second_k_send.at[t], fin_k_recv.at[t], device(0, dy, dc))

    def second_v(t, direct):
        src = pack_v if direct else mid_v
        dx, _, dc = split_slot(t)
        return remote(src.at[t], fin_v.at[t], second_v_send.at[t], fin_v_recv.at[t], device(dx, 0, dc))

    def is_final_k(t):
        return t % 8 == 0

    def is_final_v(t):
        return t // 8 == 0 and t % 2 == 0

    def nth_slot(u):
        j = (u // 2) % 4
        return ((j + 1) % 4) * 8 + ((j + u // 8 + 1) % 4) * 2 + u % 2

    order = [nth_slot(u) for u in range(N_SEQ)]

    def wanted(t):
        first = place(*split_slot(t)) * BLOCKS_DEV
        index = jnp.int32(0)
        for i in range(BLOCKS_DEV):
            entry = chart[0, first + i]
            index = jnp.maximum(index, jnp.where(entry >> 4 == seq, entry & (BLOCKS_DEV - 1), 0))
        return index

    def send_k(t, index):
        into = pack_k if t else fin_k
        into[t] = k_ref[index]
        if t // 8:
            first_k(t, is_final_k(t)).start()

    def send_v(t, index):
        into = pack_v if t else fin_v
        into[t] = v_ref[index]
        if (t // 2) % 4:
            first_v(t, is_final_v(t)).start()

    def send_slots(slots):
        for t in slots:
            index = wanted(t)
            send_k(t, index)
            send_v(t, index)

    load_k.wait()
    pl.semaphore_wait(barrier, len(peers))
    early = [(t, wanted(t)) for t in order[:4]]
    for t, index in early:
        send_k(t, index)
    load_v.wait()
    for t, index in early:
        send_v(t, index)

    q_rows = pl.ds(pl.multiple_of(x * BLOCKS_DEV, BLOCKS_DEV), BLOCKS_DEV)

    def k_rows_from(d):
        return pl.ds(pl.multiple_of((lax.rem(y + 4 - d, 4) * 2 + c) * BLOCKS_DEV, BLOCKS_DEV), BLOCKS_DEV)

    def to_other_core(d):
        rows = k_rows_from(d)
        return remote(k_sum.at[rows], k_sum.at[rows], sum_send.at[7 + d], sum_recv.at[7 + d], device(0, 0, 1))

    k_rows = k_rows_from(0)
    k_sum[k_rows, :] = jnp.sum(k_ref[...].astype(F32), axis=1)
    load_q.wait()
    q_sum[q_rows, :] = jnp.sum(q_ref[...].astype(F32), axis=1)
    sums = []
    for d in (1, 2, 3):
        sums.append(remote(q_sum.at[q_rows], q_sum.at[q_rows], sum_send.at[d], sum_recv.at[d], device(d, 0, 0)))
    for d in (1, 2, 3):
        sums.append(remote(k_sum.at[k_rows], k_sum.at[k_rows], sum_send.at[3 + d], sum_recv.at[3 + d], device(0, d, 0)))
    for copy in sums:
        copy.start()
    to_other_core(0).start()
    send_slots(order[4:12])

    def pass_slots(slots):
        for t in slots:
            dx, dy, dc = split_slot(t)
            if dx and not is_final_k(t):
                first_k(t, False).wait_recv()
            if not is_final_k(t):
                second_k(t, dx == 0).start()
            if dy and not is_final_v(t):
                first_v(t, False).wait_recv()
            if not is_final_v(t):
                second_v(t, dy == 0).start()

    turned = (((1,), (1,)), ((), ()))

    heads = [slice(h * HEAD_DIM, (h + 1) * HEAD_DIM) for h in range(GROUP_HEADS)]

    def softmax_part(keys, queries):
        scores = [lax.dot_general(k, q, turned, preferred_element_type=F32) for k, q in zip(keys, queries)]
        tops = [jnp.max(score, axis=0, keepdims=True) for score in scores]
        expos = [jnp.exp2((score - top) * (SCALE * LOG2E)) for score, top in zip(scores, tops)]
        totals = [jnp.sum(expo, axis=0, keepdims=True) for expo in expos]
        moments = [jnp.sum(expo * score, axis=0, keepdims=True) for expo, score in zip(expos, scores)]
        stack = lambda rows: jnp.concatenate(rows, axis=0)
        return expos, stack(tops) * SCALE, stack(totals), stack(moments) * SCALE

    def near_part(i):
        expos, top, total, moment = softmax_part(
            [k_ref[i, :, lanes] for lanes in heads], [q_ref[i, :, lanes] for lanes in heads]
        )
        for h in range(GROUP_HEADS):
            near_expo[i, h] = expos[h]
        near_stat[i, 0] = top
        near_stat[i, 1] = total
        near_stat[i, 2] = moment

    def near_parts(first):
        def step(u, carry):
            near_part(first + u)
            return carry

        lax.fori_loop(0, 4, step, 0)

    for d in (1, 2, 3):
        sums[2 + d].wait()
        to_other_core(d).start()
    for copy in sums[:3]:
        copy.wait()
    send_slots(order[12:16])
    for d in range(4):
        to_other_core(d).wait()
    shares = lax.dot_general(
        q_sum[...], k_sum[...], (((1,), (1,)), ((), ())), precision=lax.Precision.HIGHEST, preferred_element_type=F32
    )
    part[...] = (shares * PRICE).reshape(N_HEADS, 8, 128)
    reduces = []
    for d in range(1, N_HEADS):
        to = lax.rem(z + d, N_HEADS)
        reduces.append(remote(part.at[to], part_in.at[z], red_send.at[d], red_recv.at[d], floor(d)))
    for copy in reduces:
        copy.start()
    part_in[z] = part[z]
    send_slots(order[16:20])
    near_parts(0)
    for copy in reduces:
        copy.wait()
    cost[z, strip, x] = jnp.sum(part_in[...], axis=0)
    tiles = []
    for d in (1, 2, 3):
        tile = cost.at[z, strip, x]
        tiles.append(remote(tile, tile, tile_send.at[d], tile_recv.at[d], device(d, 0, 0)))
    for copy in tiles:
        copy.start()
    send_slots(order[20:])
    near_parts(4)
    for copy in tiles:
        copy.wait()
    tiles = []
    for d in (1, 2, 3):
        tile = cost.at[z, strip]
        tiles.append(remote(tile, tile, tile_send.at[3 + d], tile_recv.at[3 + d], device(0, d, 0)))
    for copy in tiles:
        copy.start()
    pass_slots(order[:8])
    near_parts(8)
    for copy in tiles:
        copy.wait()
    half_layer = pl.ds(c * 4, 4)
    tiles = []
    for d in range(1, N_HEADS):
        layer = cost.at[z, half_layer]
        tiles.append(remote(layer, layer, tile_send.at[10 + d], tile_recv.at[10 + d], floor(d)))
    for copy in tiles:
        copy.start()

    near_parts(12)
    pass_slots(order[8:20])
    handed = []
    for d in range(N_HEADS):
        if d:
            tiles[d - 1].wait()
        layer = cost.at[lax.rem(z + N_HEADS - d, N_HEADS), half_layer]
        copy = remote(layer, layer, tile_send.at[18 + d], tile_recv.at[18 + d], device(0, 0, 1))
        copy.start()
        handed.append(copy)
    pass_slots(order[20:])
    for copy in handed:
        copy.wait()

    col_pot[...] = jnp.zeros_like(col_pot)

    def refit(repeat, carry):
        inverse = LOG2E / soft[repeat]

        def rows(k, carry):
            scaled = cost[k] * inverse + col_pot[...][None]
            top = jnp.max(jnp.max(scaled, axis=1), axis=-1, keepdims=True)
            total = jnp.sum(jnp.sum(jnp.exp2(scaled - top[:, None]), axis=1), axis=-1, keepdims=True)
            row_pot[k] = jnp.broadcast_to(-(top + jnp.log2(total)), (8, 8, 128))
            return carry

        lax.fori_loop(0, N_HEADS, rows, 0, unroll=4)

        def tops(k, top):
            scaled = cost[k] * inverse + row_pot[k][:, None]
            return jnp.maximum(top, jnp.max(scaled, axis=0))

        top = lax.fori_loop(0, N_HEADS, tops, jnp.full((4, 8, 128), -jnp.inf, F32), unroll=2)
        top = jnp.broadcast_to(jnp.max(top, axis=1, keepdims=True), (4, 8, 128))

        def totals(k, total):
            scaled = cost[k] * inverse + row_pot[k][:, None]
            return total + jnp.sum(jnp.exp2(scaled - top[None]), axis=0)

        total = lax.fori_loop(0, N_HEADS, totals, jnp.zeros((4, 8, 128), F32), unroll=2)
        total = jnp.broadcast_to(jnp.sum(total, axis=1, keepdims=True), (4, 8, 128))
        col_pot[...] = -(top + jnp.log2(total))
        return carry

    lax.fori_loop(0, REFIT_REPEATS, refit, 0)
    inverse = LOG2E / soft[REFIT_REPEATS - 1]
    for half in range(2):
        k = x * 2 + half
        coupling = (cost[k, strip] * inverse + row_pot[k, strip][None] + col_pot[...]) * math.log(2.0) + math.log(ALL_BLOCKS)
        for column in range(4):
            mine[half * 8 : half * 8 + 8, column * 128 : column * 128 + 128] = coupling[column]

    queries = lax.broadcasted_iota(jnp.int32, (BLOCKS_DEV, 128), 0)
    partner = jnp.zeros((BLOCKS_DEV, 128), jnp.int32)
    for i in range(BLOCKS_DEV):
        partner = jnp.where(queries == i, chart[0, seq * BLOCKS_DEV + i], partner)
    partner = jnp.concatenate([partner] * 4, axis=1)
    columns = lax.broadcasted_iota(jnp.int32, (BLOCKS_DEV, ALL_BLOCKS), 1)
    biases = jnp.sum(jnp.where(columns == partner, mine[...], 0.0), axis=1, keepdims=True)
    for i in range(BLOCKS_DEV):
        near_stat[i, 3] = jnp.broadcast_to(biases[i : i + 1], (GROUP_HEADS, 128))

    def store(source):
        return pltpu.make_async_copy(out_slot.at[source], att_hbm.at[source], out_sem.at[source])

    def attend(t):
        dx, dy, dc = split_slot(t)
        source = place(4 - dx, 4 - dy, dc)
        index = jnp.int32(0)
        for i in range(BLOCKS_DEV):
            index = jnp.maximum(index, jnp.where(chart[0, seq * BLOCKS_DEV + i] >> 4 == source, i, 0))
        expos, top, total, moment = softmax_part(
            [fin_k[t, :, lanes] for lanes in heads], [q_ref[index, :, lanes] for lanes in heads]
        )
        near_top, near_total, near_moment = near_stat[index, 0], near_stat[index, 1], near_stat[index, 2]
        bias = near_stat[index, 3]
        shifted = top + bias
        joint = jnp.maximum(near_top, shifted)
        near_weight, weight = jnp.exp(near_top - joint), jnp.exp(shifted - joint)
        denominator = near_total * near_weight + total * weight
        inverse = 1.0 / denominator
        near_weight, weight = near_weight * inverse, weight * inverse
        ent_slot[source] = (
            jnp.log(denominator) + joint - (near_moment * near_weight + (moment + bias * total) * weight)
        )
        shares = [
            jnp.concatenate(
                [near_expo[index, h] * near_weight[h : h + 1], expos[h] * weight[h : h + 1]], axis=0
            ).astype(jnp.bfloat16)
            for h in range(GROUP_HEADS)
        ]
        values = [
            jnp.concatenate([v_ref[index, :, lanes], fin_v[t, :, lanes]], axis=0) for lanes in heads
        ]
        mixed = [
            lax.dot_general(p, v, (((0,), (0,)), ((), ())), preferred_element_type=F32) for p, v in zip(shares, values)
        ]
        for h, lanes in enumerate(heads):
            out_slot[source, :, lanes] = mixed[h].astype(jnp.bfloat16)
        store(source).start()

    def arrived(u, carry):
        t = nth_slot(u)

        @pl.when(t != 0)
        def _():
            second_k(t, True).wait_recv()
            second_v(t, True).wait_recv()

        attend(t)
        return carry

    lax.fori_loop(0, N_SEQ, arrived, 0)

    def stored(source, carry):
        store(source).wait()
        return carry

    lax.fori_loop(0, N_SEQ, stored, 0)

    for t in order:
        dx, dy, dc = split_slot(t)
        if dx:
            first_k(t, False).wait_send()
        if dy:
            first_v(t, False).wait_send()
        if not is_final_k(t):
            second_k(t, True).wait_send()
        if not is_final_v(t):
            second_v(t, True).wait_send()


def in_query_order(chart, att_slot, ent_slot, att_hbm, ent_ref, held, in_sem, out_sem):
    first = lax.axis_index("seq") * BLOCKS_DEV
    sources = [chart[0, first + i] >> 4 for i in range(BLOCKS_DEV)]
    copies = [pltpu.make_async_copy(att_slot.at[source], held.at[i], in_sem.at[i]) for i, source in enumerate(sources)]
    stores = [pltpu.make_async_copy(held.at[i], att_hbm.at[i], out_sem.at[i]) for i in range(BLOCKS_DEV)]
    for copy in copies:
        copy.start()
    lane = lax.broadcasted_iota(jnp.int32, (GROUP_HEADS, 128), 1)
    entropy = jnp.zeros((GROUP_HEADS, 128), F32)
    for i, source in enumerate(sources):
        mean = jnp.sum(ent_slot[source], axis=1, keepdims=True) * (1.0 / BLOCK)
        entropy = jnp.where(lane == i, mean, entropy)
    ent_ref[...] = entropy[:, :BLOCKS_DEV]
    for copy, store in zip(copies, stores):
        copy.wait()
        store.start()
    for store in stores:
        store.wait()


def on_device(queries, pile, softness, chart):
    slots = pltpu.VMEM((N_SEQ, BLOCK, WIDTH), jnp.bfloat16)
    dma = pltpu.SemaphoreType.DMA
    smem = pl.BlockSpec(memory_space=pltpu.SMEM)
    vmem = pl.BlockSpec(memory_space=pltpu.VMEM)
    hbm = pl.BlockSpec(memory_space=pl.ANY)
    att_slot, ent_slot = pl.pallas_call(
        kernel,
        out_shape=(
            jax.ShapeDtypeStruct((N_SEQ, BLOCK, WIDTH), jnp.bfloat16),
            jax.ShapeDtypeStruct((N_SEQ, GROUP_HEADS, BLOCK), F32),
        ),
        in_specs=[smem, smem, hbm, hbm],
        out_specs=(hbm, vmem),
        scratch_shapes=[
            pltpu.VMEM((BLOCKS_DEV, BLOCK, WIDTH), jnp.bfloat16),
            pltpu.VMEM((BLOCKS_DEV, BLOCK, WIDTH), jnp.bfloat16),
            pltpu.VMEM((BLOCKS_DEV, BLOCK, WIDTH), jnp.bfloat16),
            pltpu.VMEM((BLOCKS_DEV, GROUP_HEADS, BLOCK, BLOCK), F32),
            pltpu.VMEM((BLOCKS_DEV, 4, GROUP_HEADS, BLOCK), F32),
            slots, slots, slots, slots, slots, slots, slots,
            pltpu.VMEM((64, WIDTH), F32),
            pltpu.VMEM((128, WIDTH), F32),
            pltpu.VMEM((N_HEADS, 8, 128), F32),
            pltpu.VMEM((N_HEADS, 8, 128), F32),
            pltpu.VMEM((N_HEADS, 8, 4, 8, 128), F32),
            pltpu.VMEM((N_HEADS, 8, 8, 128), F32),
            pltpu.VMEM((4, 8, 128), F32),
            pltpu.VMEM((BLOCKS_DEV, ALL_BLOCKS), F32),
            dma((3,)), dma((N_SEQ,)), dma((11,)), dma((11,)), dma((8,)), dma((8,)), dma((26,)), dma((26,)),
            dma((N_SEQ,)), dma((N_SEQ,)), dma((N_SEQ,)), dma((N_SEQ,)),
            dma((N_SEQ,)), dma((N_SEQ,)), dma((N_SEQ,)), dma((N_SEQ,)),
        ],
        compiler_params=pltpu.CompilerParams(
            collective_id=0, has_side_effects=True, vmem_limit_bytes=60 * 1024 * 1024
        ),
        name="sparse_attention",
    )(
        chart, softness, queries.reshape(BLOCKS_DEV, BLOCK, WIDTH), pile.reshape(2, BLOCKS_DEV, BLOCK, WIDTH)
    )
    attended, entropy = pl.pallas_call(
        in_query_order,
        out_shape=(
            jax.ShapeDtypeStruct((BLOCKS_DEV, BLOCK, WIDTH), jnp.bfloat16),
            jax.ShapeDtypeStruct((GROUP_HEADS, BLOCKS_DEV), F32),
        ),
        in_specs=[smem, hbm, vmem],
        out_specs=(hbm, vmem),
        scratch_shapes=[pltpu.VMEM((BLOCKS_DEV, BLOCK, WIDTH), jnp.bfloat16), dma((BLOCKS_DEV,)), dma((BLOCKS_DEV,))],
        name="query_order",
    )(chart, att_slot, ent_slot)
    return attended.reshape(queries.shape), entropy


def solution(mesh):
    in_specs = (P("seq", "heads"), P(None, "seq", "heads"), P(), P("heads", None))
    out_specs = (P("seq", "heads"), P("heads", "seq"))
    return jax.shard_map(
        on_device, mesh=mesh, in_specs=in_specs, out_specs=out_specs, check_vma=False
    )
```
